32 devices in a mesh: subj: 4 (over y, x), slab: 8 (over z, core).
Axes of the slice: x: 2, y: 2, z: 4, core: 2. Of those that a mesh axis runs over, the one named last changes fastest.
Arguments:
- subjects: float32 [8, 64, 448, 128], P('subj', 'slab'), may hold values from -8 to 8
- templates: float32 [4, 64, 448, 128], P(None, 'slab', 'subj'), may hold values from -6 to 6
- labels: int32 [8], replicated, may hold values from 0 to 3, as said below
- group_live_counts: int32 [4], replicated, may hold values from 1 to 2, as said below
Outputs:
- new_templates: float32 [4, 64, 448, 128], P(None, 'slab', 'subj')
The draws below stay inside these ranges and needn't reach their ends.
Inputs may be any that keep to these rules, and one draw needn't show every extreme that they name: `labels`: slot j belongs to group j // 2; slot 0 of group g has label g mod 4. The live slots of group g are its first group_live_counts[g] slots; the other slots hold volumes of no subject; some group has all 2 slots live.
All inputs are finite; a program needn't handle non-finite values.
Results may differ from the reference program's by a relative error of at most 0.00002.
Values sent between devices are 32-bit elements; how exact they have to be, the bound alone decides.
A program may use at most 192 MiB of HBM per device.

```python
import jax
import jax.numpy as jnp
from jax import lax

TEMPLATE_COUNT = 4
RADIUS = 4
GROUP_SLOTS = 2
X = 448
Y = 128
Z = 64
GROUPS = 4
SUBJECTS = 8


def label_field(key):
    base_key = jax.random.fold_in(key, 11)
    drawn = jax.random.randint(base_key, (SUBJECTS,), 0, TEMPLATE_COUNT, dtype=jnp.int32)
    slot_positions = jnp.arange(SUBJECTS, dtype=jnp.int32)
    forced = slot_positions // GROUP_SLOTS % TEMPLATE_COUNT
    return jnp.where(slot_positions % GROUP_SLOTS == 0, forced, drawn).astype(jnp.int32)


def template_field(key):
    base_key = jax.random.fold_in(key, 23)
    return jnp.clip(jax.random.normal(base_key, (TEMPLATE_COUNT, Z, X, Y), jnp.float32), -6.0, 6.0)


def draw_templates(key, part):
    return template_field(key)


def draw_labels(key, part):
    return label_field(key)


def draw_subjects(key, part):
    cluster_ids = label_field(key)
    base_templates = template_field(key)
    gains = jax.random.uniform(jax.random.fold_in(key, 31), (SUBJECTS,), jnp.float32, 0.6, 1.4)
    noise = 0.5 * jax.random.normal(jax.random.fold_in(key, 37), (SUBJECTS, Z, X, Y), jnp.float32)
    mixed = gains[:, None, None, None] * base_templates[cluster_ids] + noise
    return jnp.clip(mixed, -8.0, 8.0)


def draw_group_live_counts(key, part):
    base_key = jax.random.fold_in(key, 41)
    first_draw = jax.random.randint(jax.random.fold_in(base_key, 1), (GROUPS,), 0, GROUP_SLOTS, dtype=jnp.int32)
    second_draw = jax.random.randint(jax.random.fold_in(base_key, 2), (GROUPS,), 0, GROUP_SLOTS, dtype=jnp.int32)
    counts = 1 + first_draw * second_draw // max(GROUP_SLOTS - 1, 1)
    busiest = jax.random.randint(jax.random.fold_in(base_key, 3), (), 0, GROUPS, dtype=jnp.int32)
    return jnp.where(jnp.arange(GROUPS, dtype=jnp.int32) == busiest, GROUP_SLOTS, counts).astype(jnp.int32)


def setup_inputs(seed: int = 0) -> dict:
    streams_of = jax.random.split(jax.random.key(seed), 5)
    subjects = draw_subjects(jax.random.fold_in(streams_of[4], 71), 0)
    templates = draw_templates(jax.random.fold_in(streams_of[4], 71), 0)
    labels = draw_labels(jax.random.fold_in(streams_of[4], 71), 0)
    group_live_counts = draw_group_live_counts(jax.random.fold_in(streams_of[4], 71), 0)
    return {"subjects": subjects, "templates": templates, "labels": labels, "group_live_counts": group_live_counts}


epsilon = 1e-5
step_size = 0.5


def window_sum(volume, which_axis, extent):
    running = lax.slice_in_dim(volume, 0, extent, axis=which_axis)
    for offset in range(1, 2 * RADIUS + 1):
        running = running + lax.slice_in_dim(volume, offset, offset + extent, axis=which_axis)
    return running


def padded_sum(volume, which_axis):
    widths = [(0, 0)] * volume.ndim
    widths[which_axis] = (RADIUS, RADIUS)
    return window_sum(jnp.pad(volume, widths), which_axis, volume.shape[which_axis])


def plane_box(volume, leading):
    return padded_sum(padded_sum(volume, leading), leading + 1)


def similarity_gradient(subject, template):
    window = float((2 * RADIUS + 1) ** 3)
    channels = jnp.stack([subject, template, subject * subject, template * template, subject * template])
    local_sums = plane_box(padded_sum(channels, 1), 2)
    subject_sum = local_sums[0]
    template_sum = local_sums[1]
    covariance = local_sums[4] - subject_sum * template_sum / window
    subject_variance = local_sums[2] - subject_sum * subject_sum / window
    template_variance = local_sums[3] - template_sum * template_sum / window
    denominator = subject_variance * template_variance + epsilon
    cross_weight = 2.0 * covariance / denominator
    spread_weight = -covariance * covariance * subject_variance / (denominator * denominator)
    mean_weight = -(cross_weight * subject_sum + 2.0 * spread_weight * template_sum) / window
    stacked = jnp.stack([mean_weight, cross_weight, spread_weight])
    filtered = plane_box(padded_sum(stacked, 1), 2)
    return filtered[0] + filtered[1] * subject + 2.0 * filtered[2] * template


def reference(subjects, templates, labels, group_live_counts):
    slot_positions = jnp.arange(SUBJECTS, dtype=jnp.int32)
    live_mask = ((slot_positions % GROUP_SLOTS) < group_live_counts[slot_positions // GROUP_SLOTS]).astype(jnp.float32)
    cluster_membership = (labels[:, None] == jnp.arange(TEMPLATE_COUNT, dtype=jnp.int32)[None, :]).astype(jnp.float32) * live_mask[:, None]
    members = jnp.sum(cluster_membership, axis=0)

    def accumulate(slot_number, cluster_totals):
        cluster_label = labels[slot_number]
        subject = lax.dynamic_index_in_dim(subjects, slot_number, 0, keepdims=False)
        template = lax.dynamic_index_in_dim(templates, cluster_label, 0, keepdims=False)
        template_gradient = similarity_gradient(subject, template)
        return cluster_totals.at[cluster_label].add(live_mask[slot_number] * template_gradient)

    cluster_totals = lax.fori_loop(0, SUBJECTS, accumulate, jnp.zeros(templates.shape, jnp.float32))
    return templates + step_size * cluster_totals / members[:, None, None, None]
```

```python
import functools

import jax
import jax.numpy as jnp
from jax import lax
from jax.experimental import pallas as pl
from jax.experimental.pallas import tpu as pltpu
from jax.sharding import PartitionSpec as P

RADIUS = 4
WIDTH = 2 * RADIUS + 1
CELLS = float(WIDTH**3)

epsilon = 1e-05
step_size = 0.5


def halo(block, axis, dim, width):
    count = lax.axis_size(axis)
    forward = [(i, i + 1) for i in range(count - 1)]
    backward = [(target, source) for source, target in forward]
    size = block.shape[dim]
    low = lax.ppermute(lax.slice_in_dim(block, size - width, size, axis=dim), axis, forward)
    high = lax.ppermute(lax.slice_in_dim(block, 0, width, axis=dim), axis, backward)
    return low, high


def thirds(value):
    high = value.astype(jnp.bfloat16)
    rest = value - high.astype(jnp.float32)
    middle = rest.astype(jnp.bfloat16)
    low = (rest - middle.astype(jnp.float32)).astype(jnp.bfloat16)
    return [high, middle, low]


def plane_box(planes, band_x, band_y):
    count = len(planes)
    rows = band_x.shape[0]
    terms = [jnp.concatenate(thirds(plane), axis=0) for plane in planes]
    along_x = [jnp.dot(band_x, term, preferred_element_type=jnp.float32) for term in terms]
    stacked = jnp.concatenate([jnp.concatenate(thirds(v), axis=1) for v in along_x], axis=0)
    summed = jnp.dot(stacked, band_y, preferred_element_type=jnp.float32)
    return [summed[i * rows : (i + 1) * rows] for i in range(count)]


def kernel(
    labels, live, low, mid, high, templates, band_1, band_2, band_y, totals, whole, sums, boxes
):
    slot = pl.program_id(0)
    clusters, extended = templates.shape[0], templates.shape[1]
    depth = mid.shape[1]
    own = totals.shape[2]
    rim = 2 * RADIUS

    @pl.when(slot == 0)
    def _():
        totals[...] = jnp.zeros_like(totals)

        def prepare(step, carry):
            k, z = step // depth, step % depth
            first = templates[k, z]
            total, square = first, first * first
            for offset in range(1, WIDTH):
                layer = templates[k, z + offset]
                total, square = total + layer, square + layer * layer
            total, square = plane_box([total, square], band_1[...], band_y[...])
            sums[k, z, 0] = total
            sums[k, z, 1] = square - total * total * (1.0 / CELLS)
            return carry

        lax.fori_loop(0, clusters * depth, prepare, 0, unroll=2)

    @pl.when(live[slot] > 0)
    def _():
        label = labels[slot]
        whole[0:RADIUS] = low[0]
        whole[RADIUS : RADIUS + depth] = mid[0]
        whole[RADIUS + depth : extended] = high[0]

        def layer(z, carry):
            s, t = whole[z], templates[label, z]
            total, square, product = s, s * s, s * t
            for offset in range(1, WIDTH):
                s, t = whole[z + offset], templates[label, z + offset]
                total, square, product = total + s, square + s * s, product + s * t
            s_sum, s_square, cross = plane_box([total, square, product], band_1[...], band_y[...])
            t_sum, t_variance = sums[label, z, 0], sums[label, z, 1]
            covariance = cross - s_sum * t_sum * (1.0 / CELLS)
            s_variance = s_square - s_sum * s_sum * (1.0 / CELLS)
            ratio = covariance / (s_variance * t_variance + epsilon)
            p = 2.0 * ratio
            q_twice = -2.0 * ratio * ratio * s_variance
            a = -(p * s_sum + q_twice * t_sum) * (1.0 / CELLS)
            result = plane_box([a, p, q_twice], band_2[...], band_y[...])
            for channel in range(3):
                boxes[z, channel] = result[channel]
            return carry

        lax.fori_loop(0, depth, layer, 0, unroll=2)

        chunk = 16 if own % 16 == 0 else 8

        def add_up(index, carry):
            start = pl.multiple_of(index * chunk, chunk)
            rows = pl.ds(start, chunk)
            inner = pl.ds(pl.multiple_of(start + rim, 8), chunk)
            for order, shift in ((range(depth), 0), (reversed(range(depth)), extended - depth)):
                running = [None] * 3
                for z in order:
                    terms = [boxes[z, channel, rows] for channel in range(3)]
                    running = [
                        new if old is None else old + new for old, new in zip(running, terms)
                    ]
                    out = z + shift
                    totals[label, out, rows] += (
                        running[0]
                        + running[1] * whole[out, inner]
                        + running[2] * templates[label, out, inner]
                    )
            return carry

        lax.fori_loop(0, own // chunk, add_up, 0)


def per_device(subjects, templates, labels, group_live_counts):
    groups = lax.axis_size("subj")
    position = lax.axis_index("subj")
    group_slots, depth, length, breadth = subjects.shape
    clusters, _, own, _ = templates.shape
    slots = labels.shape[0]
    rim = 2 * RADIUS
    rows = -(-(own + 2 * rim) // 16) * 16
    extended = depth + 2 * RADIUS

    slot_ids = jnp.arange(slots, dtype=jnp.int32)
    live = (slot_ids % group_slots < jnp.repeat(group_live_counts, group_slots)).astype(jnp.int32)
    membership = (labels[:, None] == jnp.arange(clusters, dtype=jnp.int32)[None, :]) & (
        live[:, None] > 0
    )
    members = jnp.sum(membership.astype(jnp.float32), axis=0)

    padded = jnp.pad(subjects, ((0, 0), (0, 0), (rim, rows - own - rim), (0, 0)))
    parts = jnp.stack(
        [lax.slice_in_dim(padded, i * own, i * own + rows, axis=2) for i in range(groups)]
    )
    mine = lax.all_to_all(parts, "subj", 0, 0, tiled=True).reshape(slots, depth, rows, breadth)
    s_low, s_high = halo(mine, "slab", 1, RADIUS)

    t_low, t_high = halo(templates, "slab", 1, RADIUS)
    t_deep = jnp.concatenate([t_low, templates, t_high], axis=1)
    x_low, x_high = halo(t_deep, "subj", 2, rim)
    t_whole = jnp.concatenate([x_low, t_deep, x_high], axis=2)
    if rows > own + 2 * rim:
        t_whole = jnp.pad(t_whole, ((0, 0), (0, 0), (0, rows - own - 2 * rim), (0, 0)))

    def band(out, count, inside):
        i = lax.broadcasted_iota(jnp.int32, (out, rows), 0)
        j = lax.broadcasted_iota(jnp.int32, (out, rows), 1)
        kept = (j >= i) & (j - i < WIDTH) & (i < count) & inside(j)
        return jnp.concatenate([kept.astype(jnp.bfloat16)] * 3, axis=1)

    def in_grid(j):
        x = position * own + j - RADIUS
        return (x >= 0) & (x < length)

    band_1 = band(rows, own + rim, lambda j: j >= 0)
    band_2 = band(own, own, in_grid)
    i = lax.broadcasted_iota(jnp.int32, (breadth, breadth), 0)
    j = lax.broadcasted_iota(jnp.int32, (breadth, breadth), 1)
    band_y = jnp.concatenate([(jnp.abs(i - j) <= RADIUS).astype(jnp.bfloat16)] * 3, axis=0)

    def whole_block(array):
        return pl.BlockSpec(array.shape, lambda slot, *_: (0,) * array.ndim)

    def slot_block(array):
        return pl.BlockSpec((1,) + array.shape[1:], lambda slot, *_: (slot, 0, 0, 0))

    out_shape = jax.ShapeDtypeStruct((clusters, extended, own, breadth), jnp.float32)
    totals = pl.pallas_call(
        kernel,
        grid_spec=pltpu.PrefetchScalarGridSpec(
            num_scalar_prefetch=2,
            grid=(slots,),
            in_specs=[
                slot_block(s_low),
                slot_block(mine),
                slot_block(s_high),
                whole_block(t_whole),
                whole_block(band_1),
                whole_block(band_2),
                whole_block(band_y),
            ],
            out_specs=whole_block(out_shape),
            scratch_shapes=[
                pltpu.VMEM((extended, rows, breadth), jnp.float32),
                pltpu.VMEM((clusters, depth, 2, rows, breadth), jnp.float32),
                pltpu.VMEM((depth, 3, own, breadth), jnp.float32),
            ],
        ),
        out_shape=out_shape,
        compiler_params=pltpu.CompilerParams(vmem_limit_bytes=48 * 1024 * 1024),
    )(labels, live, s_low, mine, s_high, t_whole, band_1, band_2, band_y)

    count = lax.axis_size("slab")
    forward = [(i, i + 1) for i in range(count - 1)]
    backward = [(target, source) for source, target in forward]
    from_low = lax.ppermute(totals[:, depth + RADIUS :], "slab", forward)
    from_high = lax.ppermute(totals[:, :RADIUS], "slab", backward)
    summed = totals[:, RADIUS : RADIUS + depth]
    middle = ((0, 0), (0, depth - RADIUS), (0, 0), (0, 0))
    summed = summed + jnp.pad(from_low, middle)
    summed = summed + jnp.pad(from_high, (middle[0], middle[1][::-1]) + middle[2:])
    return templates + step_size * summed / members[:, None, None, None]


def solution(mesh):
    in_specs = (P("subj", "slab", None, None), P(None, "slab", "subj", None), P(), P())
    out_specs = P(None, "slab", "subj", None)
    return jax.shard_map(
        per_device, mesh=mesh, in_specs=in_specs, out_specs=out_specs, check_vma=False
    )
```

```python
import functools

import jax
import jax.numpy as jnp
from jax import lax
from jax.experimental import pallas as pl
from jax.experimental.pallas import tpu as pltpu
from jax.sharding import PartitionSpec as P

RADIUS = 4
WIDTH = 2 * RADIUS + 1
CELLS = float(WIDTH**3)

epsilon = 1e-05
step_size = 0.5


def halo(block, axis, dim, width):
    count = lax.axis_size(axis)
    forward = [(i, i + 1) for i in range(count - 1)]
    backward = [(target, source) for source, target in forward]
    size = block.shape[dim]
    low = lax.ppermute(lax.slice_in_dim(block, size - width, size, axis=dim), axis, forward)
    high = lax.ppermute(lax.slice_in_dim(block, 0, width, axis=dim), axis, backward)
    return low, high


def thirds(value):
    high = value.astype(jnp.bfloat16)
    rest = value - high.astype(jnp.float32)
    middle = rest.astype(jnp.bfloat16)
    low = (rest - middle.astype(jnp.float32)).astype(jnp.bfloat16)
    return [high, middle, low]


def plane_box(planes, band_x, band_y):
    count = len(planes)
    rows = band_x.shape[0]
    terms = [jnp.concatenate(thirds(plane), axis=0) for plane in planes]
    along_x = [jnp.dot(band_x, term, preferred_element_type=jnp.float32) for term in terms]
    stacked = jnp.concatenate([jnp.concatenate(thirds(v), axis=1) for v in along_x], axis=0)
    summed = jnp.dot(stacked, band_y, preferred_element_type=jnp.float32)
    return [summed[i * rows : (i + 1) * rows] for i in range(count)]


def template_kernel(templates, band_1, band_y, sums):
    def prepare(z, carry):
        first = templates[0, z]
        total, square = first, first * first
        for offset in range(1, WIDTH):
            layer = templates[0, z + offset]
            total, square = total + layer, square + layer * layer
        total, square = plane_box([total, square], band_1[...], band_y[...])
        sums[0, z, 0] = total
        sums[0, z, 1] = square - total * total * (1.0 / CELLS)
        return carry

    lax.fori_loop(0, sums.shape[1], prepare, 0, unroll=2)


def kernel(labels, live, low, mid, high, templates, sums, band_1, band_2, band_y, *rest):
    given, (*outputs, whole, boxes) = rest[:-5], rest[-5:]
    slot = pl.program_id(0)
    extended = templates.shape[1]
    depth = mid.shape[1]
    own = outputs[0].shape[2]
    rim = 2 * RADIUS

    def place(out):
        if out < RADIUS:
            return outputs[0], out
        if out < RADIUS + depth:
            return outputs[1], out - RADIUS
        return outputs[2], out - RADIUS - depth

    @pl.when(slot == 0)
    def _():
        for index, output in enumerate(outputs):
            output[...] = given[index][...] if given else jnp.zeros_like(output)

    @pl.when(live[slot] > 0)
    def _():
        label = labels[slot]
        whole[0:RADIUS] = low[0]
        whole[RADIUS : RADIUS + depth] = mid[0]
        whole[RADIUS + depth : extended] = high[0]

        def layer(z, carry):
            s, t = whole[z], templates[label, z]
            total, square, product = s, s * s, s * t
            for offset in range(1, WIDTH):
                s, t = whole[z + offset], templates[label, z + offset]
                total, square, product = total + s, square + s * s, product + s * t
            s_sum, s_square, cross = plane_box([total, square, product], band_1[...], band_y[...])
            t_sum, t_variance = sums[label, z, 0], sums[label, z, 1]
            covariance = cross - s_sum * t_sum * (1.0 / CELLS)
            s_variance = s_square - s_sum * s_sum * (1.0 / CELLS)
            ratio = covariance / (s_variance * t_variance + epsilon)
            p = 2.0 * ratio
            q_twice = -2.0 * ratio * ratio * s_variance
            a = -(p * s_sum + q_twice * t_sum) * (1.0 / CELLS)
            result = plane_box([a, p, q_twice], band_2[...], band_y[...])
            for channel in range(3):
                boxes[z, channel] = result[channel]
            return carry

        lax.fori_loop(0, depth, layer, 0, unroll=2)

        chunk = 16 if own % 16 == 0 else 8

        def add_up(index, carry):
            start = pl.multiple_of(index * chunk, chunk)
            rows = pl.ds(start, chunk)
            inner = pl.ds(pl.multiple_of(start + rim, 8), chunk)
            for order, shift in ((range(depth), 0), (reversed(range(depth)), extended - depth)):
                running = [None] * 3
                for z in order:
                    terms = [boxes[z, channel, rows] for channel in range(3)]
                    running = [
                        new if old is None else old + new for old, new in zip(running, terms)
                    ]
                    out = z + shift
                    output, position = place(out)
                    output[label, position, rows] += (
                        running[0]
                        + running[1] * whole[out, inner]
                        + running[2] * templates[label, out, inner]
                    )
            return carry

        lax.fori_loop(0, own // chunk, add_up, 0)


def per_device(subjects, templates, labels, group_live_counts):
    groups = lax.axis_size("subj")
    position = lax.axis_index("subj")
    group_slots, depth, length, breadth = subjects.shape
    clusters, _, own, _ = templates.shape
    slots = labels.shape[0]
    rim = 2 * RADIUS
    rows = -(-(own + 2 * rim) // 16) * 16
    extended = depth + 2 * RADIUS

    slot_ids = jnp.arange(slots, dtype=jnp.int32)
    live = (slot_ids % group_slots < jnp.repeat(group_live_counts, group_slots)).astype(jnp.int32)
    membership = (labels[:, None] == jnp.arange(clusters, dtype=jnp.int32)[None, :]) & (
        live[:, None] > 0
    )
    members = jnp.sum(membership.astype(jnp.float32), axis=0)

    t_low, t_high = halo(templates, "slab", 1, RADIUS)
    t_deep = jnp.concatenate([t_low, templates, t_high], axis=1)
    x_low, x_high = halo(t_deep, "subj", 2, rim)
    t_whole = jnp.concatenate([x_low, t_deep, x_high], axis=2)
    if rows > own + 2 * rim:
        t_whole = jnp.pad(t_whole, ((0, 0), (0, 0), (0, rows - own - 2 * rim), (0, 0)))

    def band(out, count, inside):
        i = lax.broadcasted_iota(jnp.int32, (out, rows), 0)
        j = lax.broadcasted_iota(jnp.int32, (out, rows), 1)
        kept = (j >= i) & (j - i < WIDTH) & (i < count) & inside(j)
        return jnp.concatenate([kept.astype(jnp.bfloat16)] * 3, axis=1)

    def in_grid(j):
        x = position * own + j - RADIUS
        return (x >= 0) & (x < length)

    band_1 = band(rows, own + rim, lambda j: j >= 0)
    band_2 = band(own, own, in_grid)
    i = lax.broadcasted_iota(jnp.int32, (breadth, breadth), 0)
    j = lax.broadcasted_iota(jnp.int32, (breadth, breadth), 1)
    band_y = jnp.concatenate([(jnp.abs(i - j) <= RADIUS).astype(jnp.bfloat16)] * 3, axis=0)

    def whole_block(array):
        return pl.BlockSpec(array.shape, lambda step, *_: (0,) * array.ndim)

    def step_block(array, first=0):
        return pl.BlockSpec(
            (1,) + array.shape[1:], lambda step, *_: (step + first,) + (0,) * (array.ndim - 1)
        )

    sums_shape = jax.ShapeDtypeStruct((clusters, depth, 2, rows, breadth), jnp.float32)
    sums = pl.pallas_call(
        template_kernel,
        grid=(clusters,),
        in_specs=[step_block(t_whole), whole_block(band_1), whole_block(band_y)],
        out_specs=step_block(sums_shape),
        out_shape=sums_shape,
        compiler_params=pltpu.CompilerParams(vmem_limit_bytes=24 * 1024 * 1024),
        cost_estimate=pl.CostEstimate(
            flops=10**10, bytes_accessed=2 * t_whole.size * 4, transcendentals=0
        ),
    )(t_whole, band_1, band_y)

    def redistributed(slot):
        wide = jnp.pad(subjects[slot], ((0, 0), (rim, rows - own - rim), (0, 0)))
        parts = jnp.stack(
            [lax.slice_in_dim(wide, i * own, i * own + rows, axis=1) for i in range(groups)]
        )
        return parts

    out_shape = [
        jax.ShapeDtypeStruct((clusters, layers, own, breadth), jnp.float32)
        for layers in (RADIUS, depth, RADIUS)
    ]
    parts = [redistributed(slot) for slot in range(group_slots)]
    arrived = []
    for slot in range(group_slots):
        send = parts[slot]
        if arrived:
            send, arrived[-1] = lax.optimization_barrier((send, arrived[-1]))
        arrived.append(lax.all_to_all(send, "subj", 0, 0, tiled=True))
    calls = []
    for slot in range(group_slots):
        split = slot + 1 < group_slots and groups % 2 == 0
        size = groups // 2 if split else groups
        calls += [(slot, first, size) for first in range(0, groups, size)]
    totals = []
    for slot, first, size in calls:
        if first == 0:
            mine = arrived[slot]
            s_low, s_high = halo(mine, "slab", 1, RADIUS)
        elif slot + 1 < group_slots:
            arrived[slot + 1], *totals = lax.optimization_barrier((arrived[slot + 1], *totals))
        totals = pl.pallas_call(
            kernel,
            grid_spec=pltpu.PrefetchScalarGridSpec(
                num_scalar_prefetch=2,
                grid=(size,),
                in_specs=[step_block(v, first) for v in (s_low, mine, s_high)]
                + [whole_block(v) for v in (t_whole, sums, band_1, band_2, band_y, *totals)],
                out_specs=[whole_block(v) for v in out_shape],
                scratch_shapes=[
                    pltpu.VMEM((extended, rows, breadth), jnp.float32),
                    pltpu.VMEM((depth, 3, own, breadth), jnp.float32),
                ],
            ),
            out_shape=out_shape,
            compiler_params=pltpu.CompilerParams(vmem_limit_bytes=48 * 1024 * 1024),
            cost_estimate=pl.CostEstimate(
                flops=2 * 10**9 * size, bytes_accessed=0, transcendentals=0
            ),
        )(
            labels[slot::group_slots][first : first + size],
            live[slot::group_slots][first : first + size],
            s_low,
            mine,
            s_high,
            t_whole,
            sums,
            band_1,
            band_2,
            band_y,
            *totals,
        )

    count = lax.axis_size("slab")
    forward = [(i, i + 1) for i in range(count - 1)]
    backward = [(target, source) for source, target in forward]
    from_low = lax.ppermute(totals[2], "slab", forward)
    from_high = lax.ppermute(totals[0], "slab", backward)
    summed = totals[1]
    middle = ((0, 0), (0, depth - RADIUS), (0, 0), (0, 0))
    summed = summed + jnp.pad(from_low, middle)
    summed = summed + jnp.pad(from_high, (middle[0], middle[1][::-1]) + middle[2:])
    return templates + step_size * summed / members[:, None, None, None]


def solution(mesh):
    in_specs = (P("subj", "slab", None, None), P(None, "slab", "subj", None), P(), P())
    out_specs = P(None, "slab", "subj", None)
    return jax.shard_map(
        per_device, mesh=mesh, in_specs=in_specs, out_specs=out_specs, check_vma=False
    )
```

```python
import functools

import jax
import jax.numpy as jnp
from jax import lax
from jax.experimental import pallas as pl
from jax.experimental.pallas import tpu as pltpu
from jax.sharding import PartitionSpec as P

RADIUS = 4
WIDTH = 2 * RADIUS + 1
CELLS = float(WIDTH**3)

epsilon = 1e-05
step_size = 0.5


def halo(block, axis, dim, width):
    count = lax.axis_size(axis)
    forward = [(i, i + 1) for i in range(count - 1)]
    backward = [(target, source) for source, target in forward]
    size = block.shape[dim]
    low = lax.ppermute(lax.slice_in_dim(block, size - width, size, axis=dim), axis, forward)
    high = lax.ppermute(lax.slice_in_dim(block, 0, width, axis=dim), axis, backward)
    return low, high


def thirds(value):
    high = value.astype(jnp.bfloat16)
    rest = value - high.astype(jnp.float32)
    middle = rest.astype(jnp.bfloat16)
    low = (rest - middle.astype(jnp.float32)).astype(jnp.bfloat16)
    return [high, middle, low]


def plane_box(planes, band_x, band_y):
    count = len(planes)
    rows = band_x.shape[0]
    width = planes[0].shape[1]
    terms = [jnp.concatenate(thirds(plane), axis=0) for plane in planes]
    wide = jnp.dot(band_x, jnp.concatenate(terms, axis=1), preferred_element_type=jnp.float32)
    along_x = [wide[:, i * width : (i + 1) * width] for i in range(count)]
    stacked = jnp.concatenate([jnp.concatenate(thirds(v), axis=1) for v in along_x], axis=0)
    summed = jnp.dot(stacked, band_y, preferred_element_type=jnp.float32)
    return [summed[i * rows : (i + 1) * rows] for i in range(count)]


def template_kernel(templates, band_1, band_y, sums):
    def prepare(z, carry):
        first = templates[0, z]
        total, square = first, first * first
        for offset in range(1, WIDTH):
            layer = templates[0, z + offset]
            total, square = total + layer, square + layer * layer
        total, square = plane_box([total, square], band_1[...], band_y[...])
        sums[0, z, 0] = total
        sums[0, z, 1] = square - total * total * (1.0 / CELLS)
        return carry

    lax.fori_loop(0, sums.shape[1], prepare, 0, unroll=2)


def kernel(labels, live, low, mid, high, templates, sums, band_1, band_2, band_y, *rest):
    given, (*outputs, whole, boxes) = rest[:-5], rest[-5:]
    slot = pl.program_id(0)
    extended = templates.shape[1]
    depth = mid.shape[1]
    own = outputs[0].shape[2]
    rim = 2 * RADIUS

    def place(out):
        if out < RADIUS:
            return outputs[0], out
        if out < RADIUS + depth:
            return outputs[1], out - RADIUS
        return outputs[2], out - RADIUS - depth

    @pl.when(slot == 0)
    def _():
        for index, output in enumerate(outputs):
            output[...] = given[index][...] if given else jnp.zeros_like(output)

    @pl.when(live[slot] > 0)
    def _():
        label = labels[slot]
        whole[0:RADIUS] = low[0]
        whole[RADIUS : RADIUS + depth] = mid[0]
        whole[RADIUS + depth : extended] = high[0]

        def layer(z, carry):
            s, t = whole[z], templates[label, z]
            total, square, product = s, s * s, s * t
            for offset in range(1, WIDTH):
                s, t = whole[z + offset], templates[label, z + offset]
                total, square, product = total + s, square + s * s, product + s * t
            s_sum, s_square, cross = plane_box([total, square, product], band_1[...], band_y[...])
            t_sum, t_variance = sums[label, z, 0], sums[label, z, 1]
            covariance = cross - s_sum * t_sum * (1.0 / CELLS)
            s_variance = s_square - s_sum * s_sum * (1.0 / CELLS)
            ratio = covariance / (s_variance * t_variance + epsilon)
            p = 2.0 * ratio
            q_twice = -2.0 * ratio * ratio * s_variance
            a = -(p * s_sum + q_twice * t_sum) * (1.0 / CELLS)
            result = plane_box([a, p, q_twice], band_2[...], band_y[...])
            for channel in range(3):
                boxes[z, channel] = result[channel]
            return carry

        lax.fori_loop(0, depth, layer, 0, unroll=4)

        chunk = 16 if own % 16 == 0 else 8

        def add_up(index, carry):
            start = pl.multiple_of(index * chunk, chunk)
            rows = pl.ds(start, chunk)
            inner = pl.ds(pl.multiple_of(start + rim, 8), chunk)
            for order, shift in ((range(depth), 0), (reversed(range(depth)), extended - depth)):
                running = [None] * 3
                for z in order:
                    terms = [boxes[z, channel, rows] for channel in range(3)]
                    running = [
                        new if old is None else old + new for old, new in zip(running, terms)
                    ]
                    out = z + shift
                    output, position = place(out)
                    output[label, position, rows] += (
                        running[0]
                        + running[1] * whole[out, inner]
                        + running[2] * templates[label, out, inner]
                    )
            return carry

        lax.fori_loop(0, own // chunk, add_up, 0)


def per_device(subjects, templates, labels, group_live_counts):
    groups = lax.axis_size("subj")
    position = lax.axis_index("subj")
    group_slots, depth, length, breadth = subjects.shape
    clusters, _, own, _ = templates.shape
    slots = labels.shape[0]
    rim = 2 * RADIUS
    rows = -(-(own + 2 * rim) // 16) * 16
    extended = depth + 2 * RADIUS

    slot_ids = jnp.arange(slots, dtype=jnp.int32)
    live = (slot_ids % group_slots < jnp.repeat(group_live_counts, group_slots)).astype(jnp.int32)
    membership = (labels[:, None] == jnp.arange(clusters, dtype=jnp.int32)[None, :]) & (
        live[:, None] > 0
    )
    members = jnp.sum(membership.astype(jnp.float32), axis=0)

    t_low, t_high = halo(templates, "slab", 1, RADIUS)
    t_deep = jnp.concatenate([t_low, templates, t_high], axis=1)
    x_low, x_high = halo(t_deep, "subj", 2, rim)
    t_whole = jnp.concatenate([x_low, t_deep, x_high], axis=2)
    if rows > own + 2 * rim:
        t_whole = jnp.pad(t_whole, ((0, 0), (0, 0), (0, rows - own - 2 * rim), (0, 0)))

    def band(out, count, inside):
        i = lax.broadcasted_iota(jnp.int32, (out, rows), 0)
        j = lax.broadcasted_iota(jnp.int32, (out, rows), 1)
        kept = (j >= i) & (j - i < WIDTH) & (i < count) & inside(j)
        return jnp.concatenate([kept.astype(jnp.bfloat16)] * 3, axis=1)

    def in_grid(j):
        x = position * own + j - RADIUS
        return (x >= 0) & (x < length)

    band_1 = band(rows, own + rim, lambda j: j >= 0)
    band_2 = band(own, own, in_grid)
    i = lax.broadcasted_iota(jnp.int32, (breadth, breadth), 0)
    j = lax.broadcasted_iota(jnp.int32, (breadth, breadth), 1)
    band_y = jnp.concatenate([(jnp.abs(i - j) <= RADIUS).astype(jnp.bfloat16)] * 3, axis=0)

    def whole_block(array):
        return pl.BlockSpec(array.shape, lambda step, *_: (0,) * array.ndim)

    def step_block(array, first=0):
        return pl.BlockSpec(
            (1,) + array.shape[1:], lambda step, *_: (step + first,) + (0,) * (array.ndim - 1)
        )

    sums_shape = jax.ShapeDtypeStruct((clusters, depth, 2, rows, breadth), jnp.float32)
    sums = pl.pallas_call(
        template_kernel,
        grid=(clusters,),
        in_specs=[step_block(t_whole), whole_block(band_1), whole_block(band_y)],
        out_specs=step_block(sums_shape),
        out_shape=sums_shape,
        compiler_params=pltpu.CompilerParams(vmem_limit_bytes=24 * 1024 * 1024),
        cost_estimate=pl.CostEstimate(
            flops=10**10, bytes_accessed=2 * t_whole.size * 4, transcendentals=0
        ),
    )(t_whole, band_1, band_y)

    def redistributed(slot):
        wide = jnp.pad(subjects[slot], ((0, 0), (rim, rows - own - rim), (0, 0)))
        parts = jnp.stack(
            [lax.slice_in_dim(wide, i * own, i * own + rows, axis=1) for i in range(groups)]
        )
        return parts

    out_shape = [
        jax.ShapeDtypeStruct((clusters, layers, own, breadth), jnp.float32)
        for layers in (RADIUS, depth, RADIUS)
    ]
    parts = [redistributed(slot) for slot in range(group_slots)]
    arrived = []
    for slot in range(group_slots):
        send = parts[slot]
        if arrived:
            send, arrived[-1] = lax.optimization_barrier((send, arrived[-1]))
        arrived.append(lax.all_to_all(send, "subj", 0, 0, tiled=True))
    calls = []
    for slot in range(group_slots):
        split = slot + 1 < group_slots and groups % 2 == 0
        size = groups // 2 if split else groups
        calls += [(slot, first, size) for first in range(0, groups, size)]
    totals = []
    for slot, first, size in calls:
        if first == 0:
            mine = arrived[slot]
            s_low, s_high = halo(mine, "slab", 1, RADIUS)
        elif slot + 1 < group_slots:
            arrived[slot + 1], *totals = lax.optimization_barrier((arrived[slot + 1], *totals))
        totals = pl.pallas_call(
            kernel,
            grid_spec=pltpu.PrefetchScalarGridSpec(
                num_scalar_prefetch=2,
                grid=(size,),
                in_specs=[step_block(v, first) for v in (s_low, mine, s_high)]
                + [whole_block(v) for v in (t_whole, sums, band_1, band_2, band_y, *totals)],
                out_specs=[whole_block(v) for v in out_shape],
                scratch_shapes=[
                    pltpu.VMEM((extended, rows, breadth), jnp.float32),
                    pltpu.VMEM((depth, 3, own, breadth), jnp.float32),
                ],
            ),
            out_shape=out_shape,
            compiler_params=pltpu.CompilerParams(vmem_limit_bytes=48 * 1024 * 1024),
            cost_estimate=pl.CostEstimate(
                flops=2 * 10**9 * size, bytes_accessed=0, transcendentals=0
            ),
        )(
            labels[slot::group_slots][first : first + size],
            live[slot::group_slots][first : first + size],
            s_low,
            mine,
            s_high,
            t_whole,
            sums,
            band_1,
            band_2,
            band_y,
            *totals,
        )

    count = lax.axis_size("slab")
    forward = [(i, i + 1) for i in range(count - 1)]
    backward = [(target, source) for source, target in forward]
    from_low = lax.ppermute(totals[2], "slab", forward)
    from_high = lax.ppermute(totals[0], "slab", backward)
    summed = totals[1]
    middle = ((0, 0), (0, depth - RADIUS), (0, 0), (0, 0))
    summed = summed + jnp.pad(from_low, middle)
    summed = summed + jnp.pad(from_high, (middle[0], middle[1][::-1]) + middle[2:])
    return templates + step_size * summed / members[:, None, None, None]


def solution(mesh):
    in_specs = (P("subj", "slab", None, None), P(None, "slab", "subj", None), P(), P())
    out_specs = P(None, "slab", "subj", None)
    return jax.shard_map(
        per_device, mesh=mesh, in_specs=in_specs, out_specs=out_specs, check_vma=False
    )
```
